512 devices in a mesh: dp: 8 (over z_lo), ctx: 64 (over x, z_hi, y, core).
Axes of the slice: x: 4, y: 4, z: 16 (z_hi: 2, z_lo: 8; z = z_hi * 8 + z_lo), core: 2. Of those that a mesh axis runs over, the one named last changes fastest.
Arguments:
- query: bfloat16 [393216, 512], P(('dp', 'ctx')), parts along dimension 0, may hold values from -14 to 14
- key: bfloat16 [393216, 128], P(('dp', 'ctx')), parts along dimension 0, may hold values from -12 to 12
- value: bfloat16 [393216, 128], P(('dp', 'ctx')), parts along dimension 0, may hold values from -6 to 6
- d_out: bfloat16 [393216, 512], P(('dp', 'ctx')), parts along dimension 0, may hold values from -6 to 6
- doc_lengths: int32 [1024], P('dp'), parts along dimension 0, may hold values from 1 to 768, 49152 in all
Outputs:
- attended: bfloat16 [393216, 512], P(('dp', 'ctx')), parts along dimension 0
- d_query: bfloat16 [393216, 512], P(('dp', 'ctx')), parts along dimension 0
- d_key: bfloat16 [393216, 128], P(('dp', 'ctx')), parts along dimension 0
- d_value: bfloat16 [393216, 128], P(('dp', 'ctx')), parts along dimension 0
The draws below stay inside these ranges and needn't reach their ends.
There are 8 independent parts, one for each index of `dp`. The reference program is written for one: setup_inputs(seed, part) draws one part's arguments, and reference() takes and returns one part's arrays. A program takes and returns all parts, laid end to end along the dimension named above; each array names one. Nothing has to cross between parts.
Inputs may be any that keep to these rules, and one draw needn't show every extreme that they name: `doc_lengths`: the lengths of one session sum to 49152, and one of them is exactly 768.
All inputs are finite; a program needn't handle non-finite values.
Results may differ from the reference program's by a relative error of at most 0.035.
Values may be sent and summed in bfloat16 or wider, within the bound.
A program may use at most 64 MiB of HBM per device.

```python
import math
import jax
import jax.numpy as jnp
import numpy as np
from jax import lax

HD = 128
QH = 4
CH = 384
REACH = 2
MAXDOC = 768
L = 49152
NDOC = 128


def rough_rows(key, columns):
    values = jax.random.truncated_normal(key, -6.0, 6.0, (L, columns), jnp.float32)
    return values


def draw_query(key, part):
    values = rough_rows(jax.random.fold_in(key, 11), QH * HD)
    return values.astype(jnp.bfloat16)


def draw_key(key, part):
    values = rough_rows(jax.random.fold_in(key, 13), HD)
    return values.astype(jnp.bfloat16)


def shard_levels(key, extent, pieces, low, top_value):
    def one(position, parts):
        heights = jax.random.uniform(jax.random.fold_in(jax.random.fold_in(key, 6), position), (parts,), jnp.float32, low / len(pieces), top_value / len(pieces))
        return jnp.repeat(jnp.exp(heights), extent[position] // parts).reshape((-1,) + (1,) * (len(extent) - position - 1))

    level = one(*pieces[0])
    for cut in pieces[1:]:
        level = level * one(*cut)
    return level


def length_profile(amount, total, reach, skew):
    portions = [(1 << 20) // math.isqrt(rank ** skew) + 1 for rank in range(2, amount + 1)]
    rest, given = total - reach - (amount - 1), [1] * (amount - 1)
    while rest > 0:
        free = [i for i in range(amount - 1) if given[i] < reach]
        mass, remaining = sum([portions[i] for i in free]), rest
        for i in free:
            more = min(reach - given[i], max(1, remaining * portions[i] // mass), rest)
            given[i] = given[i] + more
            rest = rest - more
    return np.array([reach] + given)


def uneven_parts(rng, amount, total, most, skew):
    if amount == 2:
        one = jax.random.randint(rng, (), max(1, total - most), min(most, total - 1) + 1)
        return jnp.stack([one, total - one])
    lengths = jnp.asarray(length_profile(amount, total, most, skew), jnp.int32)
    twos = (amount - 1) // 2
    donor, receiver = lengths[1:1 + 2 * twos:2], lengths[2:2 + 2 * twos:2]
    slack = jnp.minimum(donor - 1, most - receiver)
    moved = jax.random.randint(jax.random.fold_in(rng, 1), (twos,), 0, 1 << 20) % (slack + 1)
    lengths = lengths.at[1:1 + 2 * twos:2].set(donor - moved).at[2:2 + 2 * twos:2].set(receiver + moved)
    return lengths[jax.random.permutation(jax.random.fold_in(rng, 2), amount)]


def bell_draw(rng, dims, scale, limit, cuts=(), kind=jnp.bfloat16):
    level = shard_levels(rng, dims, cuts, -0.22, 0.18) if cuts else 1.0
    array = jax.random.normal(rng, dims, jnp.float32) * scale * level
    return jnp.minimum(jnp.maximum(array, -limit), limit).astype(kind)


def setup_inputs(seed: int = 0, part: int = 0) -> dict:
    key_of = jax.random.split(jax.random.key(seed), 6)
    part_keys = jax.random.split(jax.random.fold_in(key_of[5], part), 6)
    query = draw_query(jax.random.fold_in(jax.random.fold_in(key_of[5], part), 71), part)
    key = draw_key(jax.random.fold_in(jax.random.fold_in(key_of[5], part), 71), part)
    value = bell_draw(part_keys[2], (L, HD), 1.0, 6.0, ((0, 64),))
    d_out = bell_draw(part_keys[3], (L, QH * HD), 1.0, 6.0, ((0, 64),))
    doc_lengths = uneven_parts(part_keys[4], NDOC, L, MAXDOC, 2).astype(jnp.int32)
    return {"query": query, "key": key, "value": value, "d_out": d_out, "doc_lengths": doc_lengths}


masked_score = -1e+30

def to_order(stored):
    count = stored.shape[0] // (2 * CH)
    blocks = stored.reshape(count, 2, CH, stored.shape[1])
    return jnp.concatenate([blocks[:, 0], blocks[::-1, 1]], axis=0).reshape(stored.shape)

def to_stored(ordered):
    count = ordered.shape[0] // (2 * CH)
    blocks = ordered.reshape(2 * count, CH, ordered.shape[1])
    return jnp.stack([blocks[:count], blocks[count:][::-1]], axis=1).reshape(ordered.shape)

def doc_index(positions, doc_lengths):
    starts = jnp.cumsum(doc_lengths) - doc_lengths
    return lax.optimization_barrier(jnp.sum((starts[None, :] <= positions[:, None]).astype(jnp.int32), axis=1)) - 1

def block_terms(query_block, dout_block, keys, values, allowed):
    scale = 1.0 / math.sqrt(HD)
    heads = query_block.shape[1] // HD
    query_heads = query_block.reshape(CH, heads, HD).astype(jnp.float32)
    dout_heads = dout_block.reshape(CH, heads, HD).astype(jnp.float32)
    keys_wide = keys.astype(jnp.float32)
    values_wide = values.astype(jnp.float32)
    scores = jnp.einsum('rhe,ke->hrk', query_heads, keys_wide) * scale
    scores = jnp.where(allowed[None], scores, masked_score)
    row_max = lax.optimization_barrier(jnp.max(scores, axis=2, keepdims=True))
    log_total = row_max + jnp.log(lax.optimization_barrier(jnp.sum(jnp.exp(scores - row_max), axis=2, keepdims=True)))
    weights = jnp.where(allowed[None], jnp.exp(scores - log_total), 0.0).astype(jnp.bfloat16)
    weights_wide = lax.optimization_barrier(weights).astype(jnp.float32)
    attended = jnp.einsum('hrk,ke->rhe', weights_wide, values_wide).astype(jnp.bfloat16)
    attended_wide = lax.optimization_barrier(attended).astype(jnp.float32)
    delta = lax.optimization_barrier(jnp.sum(dout_heads * attended_wide, axis=2))
    dprob = jnp.einsum('rhe,ke->hrk', dout_heads, values_wide)
    dscore = (weights_wide * (dprob - delta.T[:, :, None])).astype(jnp.bfloat16)
    dscore_wide = lax.optimization_barrier(dscore).astype(jnp.float32)
    grad_query = jnp.einsum('hrk,ke->rhe', dscore_wide, keys_wide) * scale
    grad_key = jnp.einsum('hrk,rhe->ke', dscore_wide, query_heads) * scale
    grad_value = jnp.einsum('hrk,rhe->ke', weights_wide, dout_heads)
    features = heads * HD
    return (attended.reshape(CH, features), grad_query.reshape(CH, features).astype(jnp.bfloat16), grad_key, grad_value)

def reference(query, key, value, d_out, doc_lengths):
    total = query.shape[0]
    features = query.shape[1]
    back = REACH * CH
    width = back + CH
    query_ord = to_order(query)
    dout_ord = to_order(d_out)
    key_pad = jnp.concatenate([jnp.zeros((back, HD), key.dtype), to_order(key)], axis=0)
    value_pad = jnp.concatenate([jnp.zeros((back, HD), value.dtype), to_order(value)], axis=0)
    positions = jnp.arange(total + back, dtype=jnp.int32) - back
    docs = doc_index(positions, doc_lengths)

    def step(carry, index):
        key_acc, value_acc = carry
        start = index * CH
        query_block = lax.dynamic_slice_in_dim(query_ord, start, CH, 0)
        dout_block = lax.dynamic_slice_in_dim(dout_ord, start, CH, 0)
        query_pos = lax.dynamic_slice_in_dim(positions, start + back, CH, 0)
        query_doc = lax.dynamic_slice_in_dim(docs, start + back, CH, 0)
        keys = lax.dynamic_slice_in_dim(key_pad, start, width, 0)
        values = lax.dynamic_slice_in_dim(value_pad, start, width, 0)
        key_pos = lax.dynamic_slice_in_dim(positions, start, width, 0)
        key_doc = lax.dynamic_slice_in_dim(docs, start, width, 0)
        allowed = (key_pos[None, :] <= query_pos[:, None]) & (key_doc[None, :] == query_doc[:, None])
        attended, grad_query, grad_key, grad_value = block_terms(query_block, dout_block, keys, values, allowed)
        key_acc = lax.dynamic_update_slice_in_dim(key_acc, lax.dynamic_slice_in_dim(key_acc, start, width, 0) + grad_key, start, 0)
        value_acc = lax.dynamic_update_slice_in_dim(value_acc, lax.dynamic_slice_in_dim(value_acc, start, width, 0) + grad_value, start, 0)
        return ((key_acc, value_acc), (attended, grad_query))
    zeros = jnp.zeros((total + back, HD), jnp.float32)
    (key_acc, value_acc), (attended, grad_query) = lax.scan(step, (zeros, zeros), jnp.arange(total // CH, dtype=jnp.int32))
    return (to_stored(attended.reshape(total, features)), to_stored(grad_query.reshape(total, features)), to_stored(key_acc[back:].astype(jnp.bfloat16)), to_stored(value_acc[back:].astype(jnp.bfloat16)))
```

```python
import math

import jax
import jax.numpy as jnp
from jax import lax
from jax.experimental import pallas as pl
from jax.experimental.pallas import tpu as pltpu
from jax.sharding import PartitionSpec as P

HD = 128
QH = 4
CH = 384
SUB = 128
WIN = 7 * SUB
OWN = 2 * CH
CHIPS = 32
MASKED = -1e30
SCALE = 1.0 / math.sqrt(HD)
SCALE2 = SCALE * math.log2(math.e)
MESH = pl.DeviceIdType.MESH
NT = (((1,), (1,)), ((), ()))
TN = (((0,), (0,)), ((), ()))
AK, AV, BK, BV, CK, CV, FK, FV, RK, RV, GA, GB, GC, GF, GR, COPIES = range(16)


def dot(a, b, dims):
    return lax.dot_general(a, b, dims, preferred_element_type=jnp.float32)


def kernel(
    q_ref, k_ref, v_ref, do_ref, len_ref,
    att_ref, dq_ref, dk_ref, dv_ref,
    kbuf, vbuf, first, acck, accv, gout, gin, gfold, relay, grelay, send, recv, fwd,
):
    d = lax.axis_index("ctx")
    c, k = d // 2, lax.rem(d, 2)
    y = lax.rem(c, 4)
    other = 1 - k
    step = 2 * k - 1
    u, w = c + step, c - step
    u2, w2 = c + 2 * step, c - 2 * step
    edge_u, edge_w = 3 * k, 3 * (1 - k)
    has_u = (u >= 0) & (u < CHIPS)
    has_w = (w >= 0) & (w < CHIPS)
    cross_u = has_u & (y == edge_u)
    cross_w = has_w & (y == edge_w)
    near_u = has_u & (y != edge_u)
    near_w = has_w & (y != edge_w)
    fold = (c == CHIPS - 1) & (k == 1)
    folded = (c == CHIPS - 1) & (k == 0)
    relay_kv = (y == edge_w + 1 - 2 * (1 - k)) & (w2 >= 0) & (w2 < CHIPS)
    relay_g = (y == edge_u + 1 - 2 * k) & (u2 >= 0) & (u2 < CHIPS)

    def at(chip, core):
        return {"ctx": chip * 2 + core}

    barrier = pltpu.get_barrier_semaphore()

    def greet(when, chip, core):
        @pl.when(when)
        def _():
            pl.semaphore_signal(barrier, inc=1, device_id=at(chip, core), device_id_type=MESH)

    pl.semaphore_signal(barrier, inc=1, device_id=at(c, other), device_id_type=MESH)
    greet(has_u, u, other)
    greet(near_u, u, k)
    greet(near_w, w, k)
    greet(cross_u, u2, k)
    greet(cross_w, w2, k)

    for slot in range(2):
        rows = slice(slot * CH, (slot + 1) * CH)
        kbuf[slot, OWN:] = k_ref[rows]
        vbuf[slot, OWN:] = v_ref[rows]

    @pl.when((c == 0) & (k == 0))
    def _():
        kbuf[0, :OWN] = jnp.zeros((OWN, HD), jnp.bfloat16)
        vbuf[0, :OWN] = jnp.zeros((OWN, HD), jnp.bfloat16)

    acck[...] = jnp.zeros_like(acck)
    accv[...] = jnp.zeros_like(accv)

    lens = jnp.broadcast_to(len_ref[...], (HD, HD))
    line = lax.broadcasted_iota(jnp.int32, (HD, HD), 0)
    lane = lax.broadcasted_iota(jnp.int32, (HD, HD), 1)
    starts = jnp.sum(
        jnp.where(lane < line, lens, 0).astype(jnp.float32), axis=1, keepdims=True
    ).astype(jnp.int32)
    for slot in range(2):
        block = d if slot == 0 else 2 * (2 * CHIPS) - 1 - d
        for sub in range(3):
            pos = block * CH + sub * SUB + lane
            held = jnp.where(starts <= pos, starts, 0)
            held = jnp.max(held.astype(jnp.float32), axis=0, keepdims=True).astype(jnp.int32)
            first[slot, sub] = jnp.broadcast_to(held - (block * CH - OWN + sub * SUB), (8, HD))

    count = (
        1
        + has_u.astype(jnp.int32)
        + near_u.astype(jnp.int32)
        + near_w.astype(jnp.int32)
        + relay_kv.astype(jnp.int32)
        + relay_g.astype(jnp.int32)
    )
    pl.semaphore_wait(barrier, count)

    def remote(src, dst, which, chip, core, out=None):
        return pltpu.make_async_remote_copy(
            src_ref=src,
            dst_ref=dst,
            send_sem=send.at[which] if out is None else out,
            recv_sem=recv.at[which],
            device_id=at(chip, core),
            device_id_type=MESH,
        )

    near, far = pl.ds(CH, CH), pl.ds(0, CH)
    mine, theirs = pl.ds(k * CH, CH), pl.ds(other * CH, CH)
    send_a = [
        remote(k_ref.at[theirs], kbuf.at[other, near], AK, u, other),
        remote(v_ref.at[theirs], vbuf.at[other, near], AV, u, other),
    ]
    send_b = [
        remote(k_ref.at[mine], kbuf.at[k, far], BK, w, k),
        remote(v_ref.at[mine], vbuf.at[k, far], BV, w, k),
    ]
    send_r = [
        remote(k_ref.at[mine], relay.at[0], RK, u, k),
        remote(v_ref.at[mine], relay.at[1], RV, u, k),
    ]
    send_c = [
        remote(k_ref.at[mine], kbuf.at[k, near], CK, c, other),
        remote(v_ref.at[mine], vbuf.at[k, near], CV, c, other),
    ]
    send_f = [
        remote(kbuf.at[k, near], kbuf.at[k, far], FK, c, other),
        remote(vbuf.at[k, near], vbuf.at[k, far], FV, c, other),
    ]
    pass_on = [
        remote(relay.at[0], kbuf.at[k, far], BK, w2, k, fwd.at[0]),
        remote(relay.at[1], vbuf.at[k, far], BV, w2, k, fwd.at[1]),
    ]
    send_ga = remote(gout.at[k, 1], gin.at[0], GA, u, other)
    send_gb = remote(gout.at[k, 0], gin.at[1], GB, u, k)
    send_gfold = remote(gout.at[k, 0], gin.at[1], GB, c, other)
    send_gr = remote(gout.at[k, 0], grelay, GR, w, k)
    send_gc = remote(gout.at[other, 1], gin.at[2], GC, c, other)
    send_gf = remote(gout.at[other, 0], gfold, GF, c, other)
    pass_g = remote(grelay, gin.at[1], GB, u2, k, fwd.at[2])

    def start(when, copies):
        @pl.when(when)
        def _():
            for copy in copies:
                copy.start()

    start(has_u, send_a)
    start(cross_w, send_r)
    start(near_w, send_b)
    for copy in send_c:
        copy.start()

    @pl.when(relay_kv)
    def _():
        for come, go in zip(send_r, pass_on):
            come.wait_recv()
            go.start()

    def landed(dst, which):
        remote(dst, dst, which, c, other).wait_recv()

    def prepare(slot):
        @pl.when(slot == k)
        def _():
            @pl.when(has_u)
            def _():
                landed(kbuf.at[k, near], AK)
                landed(vbuf.at[k, near], AV)

            @pl.when(fold)
            def _():
                kbuf[1, CH:OWN] = k_ref[:CH]
                vbuf[1, CH:OWN] = v_ref[:CH]
                kbuf[1, :CH] = kbuf[0, CH:OWN]
                vbuf[1, :CH] = vbuf[0, CH:OWN]

            for copy in send_f:
                copy.start()

            @pl.when(has_u)
            def _():
                landed(kbuf.at[k, far], BK)
                landed(vbuf.at[k, far], BV)

        @pl.when(slot == other)
        def _():
            landed(kbuf.at[other, near], CK)
            landed(vbuf.at[other, near], CV)
            landed(kbuf.at[other, far], FK)
            landed(vbuf.at[other, far], FV)

    def attend(slot):
        def tile(sub, carry):
            rows = pl.ds(pl.multiple_of(slot * CH + sub * SUB, SUB), SUB)
            window = pl.ds(pl.multiple_of(sub * SUB, SUB), WIN)
            keys = kbuf[slot, window]
            values = vbuf[slot, window]
            key_line = lax.broadcasted_iota(jnp.int32, (WIN, SUB), 0)
            query_lane = lax.broadcasted_iota(jnp.int32, (WIN, SUB), 1)
            allowed = (key_line - OWN <= query_lane) & (key_line >= first[slot, sub][:1])
            bias = jnp.where(allowed, 0.0, MASKED)
            bias = jnp.concatenate([bias, bias], axis=1)
            grad_k = grad_v = None
            for pair in range(QH // 2):
                heads = [slice(h * HD, (h + 1) * HD) for h in (2 * pair, 2 * pair + 1)]
                query = jnp.concatenate([q_ref[rows, h] for h in heads], axis=0)
                dout = jnp.concatenate([do_ref[rows, h] for h in heads], axis=0)
                scores = dot(keys, query, NT) * SCALE2 + bias
                top = jnp.max(scores, axis=0, keepdims=True)
                raised = jnp.exp2(scores - top)
                total = jnp.sum(raised, axis=0, keepdims=True)
                weights = (raised * (1.0 / total)).astype(jnp.bfloat16)
                attended = dot(weights, values, TN).astype(jnp.bfloat16)
                product = dout.astype(jnp.float32) * attended.astype(jnp.float32)
                delta = lax.dot_general(
                    jnp.ones((8, HD), jnp.float32), product, NT,
                    precision=lax.Precision.HIGHEST, preferred_element_type=jnp.float32,
                )[:1]
                dprob = dot(values, dout, NT)
                dscore = (weights.astype(jnp.float32) * (dprob - delta)).astype(jnp.bfloat16)
                grad_q = (dot(dscore, keys, TN) * SCALE).astype(jnp.bfloat16)
                for half in range(2):
                    part = slice(half * SUB, (half + 1) * SUB)
                    att_ref[rows, heads[half]] = attended[part]
                    dq_ref[rows, heads[half]] = grad_q[part]
                new_k = dot(dscore, query, (((1,), (0,)), ((), ())))
                new_v = dot(weights, dout, (((1,), (0,)), ((), ())))
                grad_k = new_k if grad_k is None else grad_k + new_k
                grad_v = new_v if grad_v is None else grad_v + new_v
            acck[slot, window] = acck[slot, window] + grad_k
            accv[slot, window] = accv[slot, window] + grad_v
            return carry

        lax.fori_loop(0, 3, tile, 0)

    def give(slot):
        @pl.when(slot == other)
        def _():
            for place in range(2):
                rows = slice(place * CH, (place + 1) * CH)
                gout[other, place, :CH] = acck[other, rows].astype(jnp.bfloat16)
                gout[other, place, CH:] = accv[other, rows].astype(jnp.bfloat16)
            send_gf.start()
            send_gc.start()

        @pl.when(slot == k)
        def _():
            gout[k, 0, :CH] = acck[k, :CH].astype(jnp.bfloat16)
            gout[k, 0, CH:] = accv[k, :CH].astype(jnp.bfloat16)
            start(near_u, [send_gb])
            start(cross_u, [send_gr])
            start(fold, [send_gfold])
            send_gf.wait_recv()
            sum_k = acck[k, CH:OWN] + gfold[:CH].astype(jnp.float32)
            sum_v = accv[k, CH:OWN] + gfold[CH:].astype(jnp.float32)

            @pl.when(has_u)
            def _():
                gout[k, 1, :CH] = sum_k.astype(jnp.bfloat16)
                gout[k, 1, CH:] = sum_v.astype(jnp.bfloat16)
                send_ga.start()

            @pl.when(fold)
            def _():
                acck[0, OWN:] = acck[0, OWN:] + sum_k
                accv[0, OWN:] = accv[0, OWN:] + sum_v

    early = (y < 2).astype(jnp.int32)

    def turn(index, carry):
        slot = early + index - 2 * early * index
        prepare(slot)
        attend(slot)
        give(slot)
        return carry

    lax.fori_loop(0, 2, turn, 0)

    @pl.when(relay_g)
    def _():
        send_gr.wait_recv()
        pass_g.start()

    def add(slot, which):
        acck[slot, OWN:] = acck[slot, OWN:] + gin[which, :CH].astype(jnp.float32)
        accv[slot, OWN:] = accv[slot, OWN:] + gin[which, CH:].astype(jnp.float32)

    send_gc.wait_recv()
    add(k, 2)

    @pl.when(has_u)
    def _():
        send_ga.wait_recv()
        add(other, 0)

    @pl.when(has_w | folded)
    def _():
        send_gb.wait_recv()
        add(k, 1)

    for slot in range(2):
        rows = slice(slot * CH, (slot + 1) * CH)
        dk_ref[rows] = (acck[slot, OWN:] * SCALE).astype(jnp.bfloat16)
        dv_ref[rows] = accv[slot, OWN:].astype(jnp.bfloat16)

    def sent(when, copies):
        @pl.when(when)
        def _():
            for copy in copies:
                copy.wait_send()

    for copy in send_c + send_f + [send_gc, send_gf]:
        copy.wait_send()
    sent(has_u, send_a + [send_ga])
    sent(near_w, send_b)
    sent(cross_w, send_r)
    sent(relay_kv, pass_on)
    sent(near_u, [send_gb])
    sent(cross_u, [send_gr])
    sent(fold, [send_gfold])
    sent(relay_g, [pass_g])


def body(query, key, value, d_out, doc_lengths):
    rows, features = query.shape
    vmem = pl.BlockSpec(memory_space=pltpu.VMEM)
    bf16, f32 = jnp.bfloat16, jnp.float32
    return pl.pallas_call(
        kernel,
        out_shape=[
            jax.ShapeDtypeStruct((rows, features), bf16),
            jax.ShapeDtypeStruct((rows, features), bf16),
            jax.ShapeDtypeStruct((rows, HD), bf16),
            jax.ShapeDtypeStruct((rows, HD), bf16),
        ],
        in_specs=[vmem] * 5,
        out_specs=[vmem] * 4,
        scratch_shapes=[
            pltpu.VMEM((2, 3 * CH, HD), bf16),
            pltpu.VMEM((2, 3 * CH, HD), bf16),
            pltpu.VMEM((2, 3, 8, HD), jnp.int32),
            pltpu.VMEM((2, 3 * CH, HD), f32),
            pltpu.VMEM((2, 3 * CH, HD), f32),
            pltpu.VMEM((2, 2, 2 * CH, HD), bf16),
            pltpu.VMEM((3, 2 * CH, HD), bf16),
            pltpu.VMEM((2 * CH, HD), bf16),
            pltpu.VMEM((2, CH, HD), bf16),
            pltpu.VMEM((2 * CH, HD), bf16),
            pltpu.SemaphoreType.DMA((COPIES,)),
            pltpu.SemaphoreType.DMA((COPIES,)),
            pltpu.SemaphoreType.DMA((3,)),
        ],
        compiler_params=pltpu.CompilerParams(
            collective_id=0, has_side_effects=True, vmem_limit_bytes=48 * 2**20
        ),
        cost_estimate=pl.CostEstimate(
            flops=4_300_000_000, bytes_accessed=4_000_000, transcendentals=2_800_000
        ),
    )(query, key, value, d_out, doc_lengths.reshape(1, -1))


def solution(mesh):
    wide = P(("dp", "ctx"), None)
    return jax.shard_map(
        body,
        mesh=mesh,
        in_specs=(wide, wide, wide, wide, P("dp")),
        out_specs=(wide, wide, wide, wide),
        check_vma=False,
    )
```

```python
import math

import jax
import jax.numpy as jnp
from jax import lax
from jax.experimental import pallas as pl
from jax.experimental.pallas import tpu as pltpu
from jax.sharding import PartitionSpec as P

HD = 128
QH = 4
CH = 384
SUB = 128
WIN = 7 * SUB
OWN = 2 * CH
CHIPS = 32
MASKED = -1e30
SCALE = 1.0 / math.sqrt(HD)
SCALE2 = SCALE * math.log2(math.e)
MESH = pl.DeviceIdType.MESH
NN = (((1,), (0,)), ((), ()))
AK, AV, BK, BV, CK, CV, FK, FV, RK, RV, GA, GB, HB, GC, GF, GR, HR, COPIES = range(18)


def dot(a, b, dims):
    return lax.dot_general(a, b, dims, preferred_element_type=jnp.float32)


def kernel(
    q_hbm, k_hbm, v_hbm, do_hbm, len_ref,
    att_hbm, dq_hbm, dk_hbm, dv_hbm,
    q_ref, do_ref, att_ref, dq_ref, dk_ref, dv_ref, kbuf, vbuf, first, acck, accv,
    gout, gin, gfold, relay, grelay, send, recv, fwd, load, save,
):
    d = lax.axis_index("ctx")
    c, k = d // 2, lax.rem(d, 2)
    y = lax.rem(c, 4)
    other = 1 - k
    step = 2 * k - 1
    u, w = c + step, c - step
    u2, w2 = c + 2 * step, c - 2 * step
    edge_u, edge_w = 3 * k, 3 * (1 - k)
    has_u = (u >= 0) & (u < CHIPS)
    has_w = (w >= 0) & (w < CHIPS)
    cross_u = has_u & (y == edge_u)
    cross_w = has_w & (y == edge_w)
    near_u = has_u & (y != edge_u)
    near_w = has_w & (y != edge_w)
    fold = (c == CHIPS - 1) & (k == 1)
    folded = (c == CHIPS - 1) & (k == 0)
    relay_kv = (y == edge_w + 1 - 2 * (1 - k)) & (w2 >= 0) & (w2 < CHIPS)
    relay_g = (y == edge_u + 1 - 2 * k) & (u2 >= 0) & (u2 < CHIPS)

    def at(chip, core):
        return {"ctx": chip * 2 + core}

    barrier = pltpu.get_barrier_semaphore()

    def greet(when, chip, core):
        @pl.when(when)
        def _():
            pl.semaphore_signal(barrier, inc=1, device_id=at(chip, core), device_id_type=MESH)

    pl.semaphore_signal(barrier, inc=1, device_id=at(c, other), device_id_type=MESH)
    greet(has_u, u, other)
    greet(near_u, u, k)
    greet(near_w, w, k)
    greet(cross_u, u2, k)
    greet(cross_w, w2, k)

    loads = [
        pltpu.make_async_copy(q_hbm, q_ref, load.at[0]),
        pltpu.make_async_copy(do_hbm, do_ref, load.at[1]),
    ]
    for slot in range(2):
        rows, place = pl.ds(slot * CH, CH), pl.ds(OWN, CH)
        loads += [
            pltpu.make_async_copy(k_hbm.at[rows], kbuf.at[slot, place], load.at[2 + 2 * slot]),
            pltpu.make_async_copy(v_hbm.at[rows], vbuf.at[slot, place], load.at[3 + 2 * slot]),
        ]
    for copy in loads:
        copy.start()

    @pl.when((c == 0) & (k == 0))
    def _():
        kbuf[0, :OWN] = jnp.zeros((OWN, HD), jnp.bfloat16)
        vbuf[0, :OWN] = jnp.zeros((OWN, HD), jnp.bfloat16)

    acck[...] = jnp.zeros_like(acck)
    accv[...] = jnp.zeros_like(accv)

    lens = jnp.broadcast_to(len_ref[...], (HD, HD))
    line = lax.broadcasted_iota(jnp.int32, (HD, HD), 0)
    lane = lax.broadcasted_iota(jnp.int32, (HD, HD), 1)
    starts = jnp.sum(
        jnp.where(lane < line, lens, 0).astype(jnp.float32), axis=1, keepdims=True
    ).astype(jnp.int32)
    for slot in range(2):
        block = d if slot == 0 else 2 * (2 * CHIPS) - 1 - d
        for sub in range(3):
            pos = block * CH + sub * SUB + lane
            held = jnp.where(starts <= pos, starts, 0)
            held = jnp.max(held.astype(jnp.float32), axis=0, keepdims=True).astype(jnp.int32)
            first[slot, sub] = jnp.broadcast_to(held - (block * CH - OWN + sub * SUB), (8, HD))

    count = (
        1
        + has_u.astype(jnp.int32)
        + near_u.astype(jnp.int32)
        + near_w.astype(jnp.int32)
        + relay_kv.astype(jnp.int32)
        + relay_g.astype(jnp.int32)
    )
    pl.semaphore_wait(barrier, count)

    def remote(src, dst, which, chip, core, out=None):
        return pltpu.make_async_remote_copy(
            src_ref=src,
            dst_ref=dst,
            send_sem=send.at[which] if out is None else out,
            recv_sem=recv.at[which],
            device_id=at(chip, core),
            device_id_type=MESH,
        )

    near, far = pl.ds(CH, CH), pl.ds(0, CH)
    mine, theirs = pl.ds(k * CH, CH), pl.ds(other * CH, CH)
    send_a = [
        remote(k_hbm.at[theirs], kbuf.at[other, near], AK, u, other),
        remote(v_hbm.at[theirs], vbuf.at[other, near], AV, u, other),
    ]
    send_b = [
        remote(k_hbm.at[mine], kbuf.at[k, far], BK, w, k),
        remote(v_hbm.at[mine], vbuf.at[k, far], BV, w, k),
    ]
    send_r = [
        remote(k_hbm.at[mine], relay.at[0], RK, u, k),
        remote(v_hbm.at[mine], relay.at[1], RV, u, k),
    ]
    send_c = [
        remote(k_hbm.at[mine], kbuf.at[k, near], CK, c, other),
        remote(v_hbm.at[mine], vbuf.at[k, near], CV, c, other),
    ]
    send_f = [
        remote(kbuf.at[k, near], kbuf.at[k, far], FK, c, other),
        remote(vbuf.at[k, near], vbuf.at[k, far], FV, c, other),
    ]
    pass_on = [
        remote(relay.at[0], kbuf.at[k, far], BK, w2, k, fwd.at[0]),
        remote(relay.at[1], vbuf.at[k, far], BV, w2, k, fwd.at[1]),
    ]
    send_ga = remote(gout.at[k, 1], gin.at[0], GA, u, other)
    halves = [pl.ds(0, CH), pl.ds(CH, CH)]
    send_gb = [remote(gout.at[k, 0, h], gin.at[1, h], GB + i, u, k) for i, h in enumerate(halves)]
    send_gfold = [
        remote(gout.at[k, 0, h], gin.at[1, h], GB + i, c, other) for i, h in enumerate(halves)
    ]
    send_gr = [remote(gout.at[k, 0, h], grelay.at[h], GR + i, w, k) for i, h in enumerate(halves)]
    send_gc = remote(gout.at[other, 1], gin.at[2], GC, c, other)
    send_gf = remote(gout.at[other, 0], gfold, GF, c, other)
    pass_g = [
        remote(grelay.at[h], gin.at[1, h], GB + i, u2, k, fwd.at[2 + i])
        for i, h in enumerate(halves)
    ]

    def start(when, copies):
        @pl.when(when)
        def _():
            for copy in copies:
                copy.start()

    start(has_u, send_a)
    start(cross_w, send_r)
    start(near_w, send_b)
    for copy in send_c:
        copy.start()

    @pl.when(relay_kv)
    def _():
        for come, go in zip(send_r, pass_on):
            come.wait_recv()
            go.start()

    def landed(dst, which):
        remote(dst, dst, which, c, other).wait_recv()

    def prepare(slot):
        @pl.when(slot == k)
        def _():
            @pl.when(fold)
            def _():
                kbuf[1, CH:OWN] = kbuf[0, OWN:]
                vbuf[1, CH:OWN] = vbuf[0, OWN:]
                kbuf[1, :CH] = kbuf[0, CH:OWN]
                vbuf[1, :CH] = vbuf[0, CH:OWN]

            @pl.when(has_u)
            def _():
                landed(kbuf.at[k, near], AK)

            send_f[0].start()

            @pl.when(has_u)
            def _():
                landed(vbuf.at[k, near], AV)

            send_f[1].start()

            @pl.when(has_u)
            def _():
                landed(kbuf.at[k, far], BK)
                landed(vbuf.at[k, far], BV)

        @pl.when(slot == other)
        def _():
            landed(kbuf.at[other, near], CK)
            landed(vbuf.at[other, near], CV)
            landed(kbuf.at[other, far], FK)
            landed(vbuf.at[other, far], FV)

    def attend(slot):
        def tile(sub, carry):
            rows = pl.ds(pl.multiple_of(slot * CH + sub * SUB, SUB), SUB)
            window = pl.ds(pl.multiple_of(sub * SUB, SUB), WIN)
            keys = kbuf[slot, window]
            values = vbuf[slot, window]
            key_line = lax.broadcasted_iota(jnp.int32, (WIN, SUB), 0)
            query_lane = lax.broadcasted_iota(jnp.int32, (WIN, SUB), 1)
            allowed = (key_line - OWN <= query_lane) & (key_line >= first[slot, sub][:1])
            bias = jnp.concatenate([jnp.where(allowed, 0.0, MASKED)] * QH, axis=1)
            heads = [slice(h * HD, (h + 1) * HD) for h in range(QH)]
            query = jnp.concatenate([q_ref[rows, h] for h in heads], axis=0)
            dout = jnp.concatenate([do_ref[rows, h] for h in heads], axis=0)
            dout_t = dout.T
            scores = dot(keys, query.T, NN) * SCALE2 + bias
            top = jnp.max(scores, axis=0, keepdims=True)
            raised = jnp.exp2(scores - top)
            total = jnp.sum(raised, axis=0, keepdims=True)
            weights = (raised * (1.0 / total)).astype(jnp.bfloat16)
            attended = dot(values.T, weights, NN).astype(jnp.bfloat16)
            delta = jnp.sum(
                dout_t.astype(jnp.float32) * attended.astype(jnp.float32), axis=0, keepdims=True
            )
            dprob = dot(values, dout_t, NN)
            dscore = (weights.astype(jnp.float32) * (dprob - delta)).astype(jnp.bfloat16)
            grad_q = (dot(keys.T, dscore, NN) * SCALE).astype(jnp.bfloat16).T
            attended = attended.T
            for h in range(QH):
                part = slice(h * SUB, (h + 1) * SUB)
                att_ref[rows, heads[h]] = attended[part]
                dq_ref[rows, heads[h]] = grad_q[part]
            acck[slot, window] = acck[slot, window] + dot(dscore, query, NN)
            accv[slot, window] = accv[slot, window] + dot(weights, dout, NN)
            return carry

        lax.fori_loop(0, 3, tile, 0, unroll=3)

    def give(slot):
        @pl.when(slot == other)
        def _():
            for place in range(2):
                rows = slice(place * CH, (place + 1) * CH)
                gout[other, place, :CH] = acck[other, rows].astype(jnp.bfloat16)
                gout[other, place, CH:] = accv[other, rows].astype(jnp.bfloat16)
            send_gf.start()
            send_gc.start()

        @pl.when(slot == k)
        def _():
            gout[k, 0, :CH] = acck[k, :CH].astype(jnp.bfloat16)
            gout[k, 0, CH:] = accv[k, :CH].astype(jnp.bfloat16)
            start(near_u, send_gb)
            start(cross_u, send_gr)
            start(fold, send_gfold)
            send_gf.wait_recv()
            sum_k = acck[k, CH:OWN] + gfold[:CH].astype(jnp.float32)
            sum_v = accv[k, CH:OWN] + gfold[CH:].astype(jnp.float32)

            @pl.when(has_u)
            def _():
                gout[k, 1, :CH] = sum_k.astype(jnp.bfloat16)
                gout[k, 1, CH:] = sum_v.astype(jnp.bfloat16)
                send_ga.start()

            @pl.when(fold)
            def _():
                acck[0, OWN:] = acck[0, OWN:] + sum_k
                accv[0, OWN:] = accv[0, OWN:] + sum_v

    for copy in loads:
        copy.wait()

    def saves(slot):
        rows = pl.ds(slot * CH, CH)
        return [
            pltpu.make_async_copy(att_ref.at[rows], att_hbm.at[rows], save.at[2 * slot]),
            pltpu.make_async_copy(dq_ref.at[rows], dq_hbm.at[rows], save.at[2 * slot + 1]),
        ]

    early = (y < 2).astype(jnp.int32)

    def turn(index, carry):
        slot = early + index - 2 * early * index
        prepare(slot)
        attend(slot)
        give(slot)
        for copy in saves(slot):
            copy.start()
        return carry

    lax.fori_loop(0, 2, turn, 0)

    @pl.when(relay_g)
    def _():
        for come, go in zip(send_gr, pass_g):
            come.wait_recv()
            go.start()

    def add(slot, which):
        acck[slot, OWN:] = acck[slot, OWN:] + gin[which, :CH].astype(jnp.float32)
        accv[slot, OWN:] = accv[slot, OWN:] + gin[which, CH:].astype(jnp.float32)

    send_gc.wait_recv()
    add(k, 2)

    @pl.when(has_u)
    def _():
        send_ga.wait_recv()
        add(other, 0)

    @pl.when(has_w | folded)
    def _():
        for copy in send_gb:
            copy.wait_recv()
        add(k, 1)

    for slot in range(2):
        rows = slice(slot * CH, (slot + 1) * CH)
        dk_ref[rows] = (acck[slot, OWN:] * SCALE).astype(jnp.bfloat16)
        dv_ref[rows] = accv[slot, OWN:].astype(jnp.bfloat16)

    last = [
        pltpu.make_async_copy(dk_ref, dk_hbm, save.at[4]),
        pltpu.make_async_copy(dv_ref, dv_hbm, save.at[5]),
    ]
    for copy in last:
        copy.start()

    def sent(when, copies):
        @pl.when(when)
        def _():
            for copy in copies:
                copy.wait_send()

    for copy in send_c + send_f + [send_gc, send_gf]:
        copy.wait_send()
    sent(has_u, send_a + [send_ga])
    sent(near_w, send_b)
    sent(cross_w, send_r)
    sent(relay_kv, pass_on)
    sent(near_u, send_gb)
    sent(cross_u, send_gr)
    sent(fold, send_gfold)
    sent(relay_g, pass_g)
    for copy in saves(0) + saves(1) + last:
        copy.wait()


def write(*refs):
    sources, outs, held, came, done = refs[:4], refs[4:8], refs[8:12], refs[12], refs[13]
    loads = [
        pltpu.make_async_copy(src, buf, came.at[i])
        for i, (src, buf) in enumerate(zip(sources, held))
    ]
    copies = [
        pltpu.make_async_copy(buf, out, done.at[i])
        for i, (buf, out) in enumerate(zip(held, outs))
    ]
    for copy in loads:
        copy.start()
    for load, copy in zip(loads, copies):
        load.wait()
        copy.start()
    for copy in copies:
        copy.wait()


def body(query, key, value, d_out, doc_lengths):
    rows, features = query.shape
    vmem = pl.BlockSpec(memory_space=pltpu.VMEM)
    hbm = pl.BlockSpec(memory_space=pltpu.HBM)
    bf16, f32 = jnp.bfloat16, jnp.float32
    shapes = [
        jax.ShapeDtypeStruct((rows, features), bf16),
        jax.ShapeDtypeStruct((rows, features), bf16),
        jax.ShapeDtypeStruct((rows, HD), bf16),
        jax.ShapeDtypeStruct((rows, HD), bf16),
    ]
    made = pl.pallas_call(
        kernel,
        out_shape=shapes,
        in_specs=[hbm] * 4 + [vmem],
        out_specs=[hbm] * 4,
        scratch_shapes=[
            *[pltpu.VMEM((rows, features), bf16)] * 4,
            *[pltpu.VMEM((rows, HD), bf16)] * 2,
            pltpu.VMEM((2, 3 * CH, HD), bf16),
            pltpu.VMEM((2, 3 * CH, HD), bf16),
            pltpu.VMEM((2, 3, 8, HD), jnp.int32),
            pltpu.VMEM((2, 3 * CH, HD), f32),
            pltpu.VMEM((2, 3 * CH, HD), f32),
            pltpu.VMEM((2, 2, 2 * CH, HD), bf16),
            pltpu.VMEM((3, 2 * CH, HD), bf16),
            pltpu.VMEM((2 * CH, HD), bf16),
            pltpu.VMEM((2, CH, HD), bf16),
            pltpu.VMEM((2 * CH, HD), bf16),
            pltpu.SemaphoreType.DMA((COPIES,)),
            pltpu.SemaphoreType.DMA((COPIES,)),
            pltpu.SemaphoreType.DMA((4,)),
            pltpu.SemaphoreType.DMA((6,)),
            pltpu.SemaphoreType.DMA((6,)),
        ],
        compiler_params=pltpu.CompilerParams(
            collective_id=0, has_side_effects=True, vmem_limit_bytes=60_000_000
        ),
        cost_estimate=pl.CostEstimate(
            flops=4_300_000_000, bytes_accessed=4_000_000, transcendentals=2_800_000
        ),
    )(query, key, value, d_out, doc_lengths.reshape(1, -1))
    return pl.pallas_call(
        write,
        out_shape=shapes,
        in_specs=[hbm] * 4,
        out_specs=[hbm] * 4,
        scratch_shapes=[
            *[pltpu.VMEM(shape.shape, bf16) for shape in shapes],
            pltpu.SemaphoreType.DMA((4,)),
            pltpu.SemaphoreType.DMA((4,)),
        ],
        compiler_params=pltpu.CompilerParams(vmem_limit_bytes=60_000_000),
        cost_estimate=pl.CostEstimate(flops=0, bytes_accessed=4_000_000, transcendentals=0),
    )(*made)


def solution(mesh):
    wide = P(("dp", "ctx"), None)
    return jax.shard_map(
        body,
        mesh=mesh,
        in_specs=(wide, wide, wide, wide, P("dp")),
        out_specs=(wide, wide, wide, wide),
        check_vma=False,
    )
```

```python
import math

import jax
import jax.numpy as jnp
from jax import lax
from jax.experimental import pallas as pl
from jax.experimental.pallas import tpu as pltpu
from jax.sharding import PartitionSpec as P

HD = 128
QH = 4
CH = 384
SUB = 128
WIN = 7 * SUB
OWN = 2 * CH
CHIPS = 32
MASKED = -1e30
SCALE = 1.0 / math.sqrt(HD)
SCALE2 = SCALE * math.log2(math.e)
LATER = (3, 5, 8)
MESH = pl.DeviceIdType.MESH
NN = (((1,), (0,)), ((), ()))
AK, AV, BK, BV, CK, CV, FK, FV, RK, RV, GA, GB, HB, GC, GF, GR, HR, COPIES = range(18)


def dot(a, b, dims):
    return lax.dot_general(a, b, dims, preferred_element_type=jnp.float32)


def kernel(
    q_hbm, k_hbm, v_hbm, do_hbm, len_ref,
    att_hbm, dq_hbm, dk_hbm, dv_hbm,
    q_ref, do_ref, att_ref, dq_ref, dk_ref, dv_ref, kbuf, vbuf, first, acck, accv,
    wbuf, delta, turned, accq, gout, gin, gfold, relay, grelay, send, recv, fwd, load, save,
):
    d = lax.axis_index("ctx")
    c, k = d // 2, lax.rem(d, 2)
    y = lax.rem(c, 4)
    other = 1 - k
    step = 2 * k - 1
    u, w = c + step, c - step
    u2, w2 = c + 2 * step, c - 2 * step
    edge_u, edge_w = 3 * k, 3 * (1 - k)
    has_u = (u >= 0) & (u < CHIPS)
    has_w = (w >= 0) & (w < CHIPS)
    cross_u = has_u & (y == edge_u)
    cross_w = has_w & (y == edge_w)
    near_u = has_u & (y != edge_u)
    near_w = has_w & (y != edge_w)
    fold = (c == CHIPS - 1) & (k == 1)
    folded = (c == CHIPS - 1) & (k == 0)
    relay_kv = (y == edge_w + 1 - 2 * (1 - k)) & (w2 >= 0) & (w2 < CHIPS)
    relay_g = (y == edge_u + 1 - 2 * k) & (u2 >= 0) & (u2 < CHIPS)

    def at(chip, core):
        return {"ctx": chip * 2 + core}

    barrier = pltpu.get_barrier_semaphore()

    def greet(when, chip, core):
        @pl.when(when)
        def _():
            pl.semaphore_signal(barrier, inc=1, device_id=at(chip, core), device_id_type=MESH)

    pl.semaphore_signal(barrier, inc=1, device_id=at(c, other), device_id_type=MESH)
    greet(has_u, u, other)
    greet(near_u, u, k)
    greet(near_w, w, k)
    greet(cross_u, u2, k)
    greet(cross_w, w2, k)

    loads = [
        pltpu.make_async_copy(q_hbm, q_ref, load.at[0]),
        pltpu.make_async_copy(do_hbm, do_ref, load.at[1]),
    ]
    for slot in range(2):
        rows, place = pl.ds(slot * CH, CH), pl.ds(OWN, CH)
        loads += [
            pltpu.make_async_copy(k_hbm.at[rows], kbuf.at[slot, place], load.at[2 + 2 * slot]),
            pltpu.make_async_copy(v_hbm.at[rows], vbuf.at[slot, place], load.at[3 + 2 * slot]),
        ]
    for copy in loads:
        copy.start()

    @pl.when((c == 0) & (k == 0))
    def _():
        kbuf[0, :OWN] = jnp.zeros((OWN, HD), jnp.bfloat16)
        vbuf[0, :OWN] = jnp.zeros((OWN, HD), jnp.bfloat16)

    lens = jnp.broadcast_to(len_ref[...], (HD, HD))
    line = lax.broadcasted_iota(jnp.int32, (HD, HD), 0)
    lane = lax.broadcasted_iota(jnp.int32, (HD, HD), 1)
    starts = jnp.sum(
        jnp.where(lane < line, lens, 0).astype(jnp.float32), axis=1, keepdims=True
    ).astype(jnp.int32)
    for slot in range(2):
        block = d if slot == 0 else 2 * (2 * CHIPS) - 1 - d
        for sub in range(3):
            pos = block * CH + sub * SUB + lane
            held = jnp.where(starts <= pos, starts, 0)
            held = jnp.max(held.astype(jnp.float32), axis=0, keepdims=True).astype(jnp.int32)
            first[slot, sub] = jnp.broadcast_to(held - (block * CH - OWN + sub * SUB), (8, HD))

    count = (
        1
        + has_u.astype(jnp.int32)
        + near_u.astype(jnp.int32)
        + near_w.astype(jnp.int32)
        + relay_kv.astype(jnp.int32)
        + relay_g.astype(jnp.int32)
    )
    pl.semaphore_wait(barrier, count)

    def remote(src, dst, which, chip, core, out=None):
        return pltpu.make_async_remote_copy(
            src_ref=src,
            dst_ref=dst,
            send_sem=send.at[which] if out is None else out,
            recv_sem=recv.at[which],
            device_id=at(chip, core),
            device_id_type=MESH,
        )

    near, far = pl.ds(CH, CH), pl.ds(0, CH)
    mine, theirs = pl.ds(k * CH, CH), pl.ds(other * CH, CH)
    send_a = [
        remote(k_hbm.at[theirs], kbuf.at[other, near], AK, u, other),
        remote(v_hbm.at[theirs], vbuf.at[other, near], AV, u, other),
    ]
    send_b = [
        remote(k_hbm.at[mine], kbuf.at[k, far], BK, w, k),
        remote(v_hbm.at[mine], vbuf.at[k, far], BV, w, k),
    ]
    send_r = [
        remote(k_hbm.at[mine], relay.at[0], RK, u, k),
        remote(v_hbm.at[mine], relay.at[1], RV, u, k),
    ]
    send_c = [
        remote(k_hbm.at[mine], kbuf.at[k, near], CK, c, other),
        remote(v_hbm.at[mine], vbuf.at[k, near], CV, c, other),
    ]
    send_f = [
        remote(kbuf.at[k, near], kbuf.at[k, far], FK, c, other),
        remote(vbuf.at[k, near], vbuf.at[k, far], FV, c, other),
    ]
    pass_on = [
        remote(relay.at[0], kbuf.at[k, far], BK, w2, k, fwd.at[0]),
        remote(relay.at[1], vbuf.at[k, far], BV, w2, k, fwd.at[1]),
    ]
    send_ga = remote(gout.at[k, 1], gin.at[0], GA, u, other)
    halves = [pl.ds(0, CH), pl.ds(CH, CH)]
    send_gb = [remote(gout.at[k, 0, h], gin.at[1, h], GB + i, u, k) for i, h in enumerate(halves)]
    send_gfold = [
        remote(gout.at[k, 0, h], gin.at[1, h], GB + i, c, other) for i, h in enumerate(halves)
    ]
    send_gr = [remote(gout.at[k, 0, h], grelay.at[h], GR + i, w, k) for i, h in enumerate(halves)]
    send_gc = remote(gout.at[other, 1], gin.at[2], GC, c, other)
    send_gf = remote(gout.at[other, 0], gfold, GF, c, other)
    pass_g = [
        remote(grelay.at[h], gin.at[1, h], GB + i, u2, k, fwd.at[2 + i])
        for i, h in enumerate(halves)
    ]

    def start(when, copies):
        @pl.when(when)
        def _():
            for copy in copies:
                copy.start()

    z_low = lax.axis_index("dp")
    group = sum((z_low >= bound).astype(jnp.int32) for bound in LATER)

    def send_far(when):
        start(cross_u & when, send_a)

        @pl.when(relay_kv & when)
        def _():
            for come, go in zip(send_r, pass_on):
                come.wait_recv()
                go.start()

    start(near_u, send_a)
    start(cross_w, send_r)
    start(near_w, send_b)
    for copy in send_c:
        copy.start()
    send_far(group == 0)

    def landed(dst, which):
        remote(dst, dst, which, c, other).wait_recv()

    def arrive(slot, buf, copy_f, which):
        of_a, of_b, of_c, of_f = which

        @pl.when(slot == k)
        def _():
            @pl.when(fold)
            def _():
                buf[1, CH:OWN] = buf[0, OWN:]
                buf[1, :CH] = buf[0, CH:OWN]

            @pl.when(has_u)
            def _():
                landed(buf.at[k, near], of_a)

            copy_f.start()

            @pl.when(has_u)
            def _():
                landed(buf.at[k, far], of_b)

        @pl.when(slot == other)
        def _():
            landed(buf.at[other, near], of_c)
            landed(buf.at[other, far], of_f)

    def head_rows(ref, slot, sub):
        rows = pl.ds(pl.multiple_of(slot * CH + sub * SUB, SUB), SUB)
        return jnp.concatenate([ref[rows, h * HD : (h + 1) * HD] for h in range(QH)], axis=0)

    def store_heads(ref, slot, sub, value):
        rows = pl.ds(pl.multiple_of(slot * CH + sub * SUB, SUB), SUB)
        for h in range(QH):
            ref[rows, h * HD : (h + 1) * HD] = value[h * SUB : (h + 1) * SUB]

    def weigh(slot):
        for sub in range(3):
            keys = kbuf[slot, sub * SUB : sub * SUB + WIN]
            key_line = lax.broadcasted_iota(jnp.int32, (WIN, SUB), 0)
            query_lane = lax.broadcasted_iota(jnp.int32, (WIN, SUB), 1)
            allowed = (key_line - OWN <= query_lane) & (key_line >= first[slot, sub][:1])
            bias = jnp.concatenate([jnp.where(allowed, 0.0, MASKED)] * QH, axis=1)
            scores = dot(keys, head_rows(q_ref, slot, sub).T, NN) * SCALE2 + bias
            top = jnp.max(scores, axis=0, keepdims=True)
            raised = jnp.exp2(scores - top)
            total = jnp.sum(raised, axis=0, keepdims=True)
            wbuf[sub] = (raised * (1.0 / total)).astype(jnp.bfloat16)

    def attend(slot):
        for sub in range(3):
            values = vbuf[slot, sub * SUB : sub * SUB + WIN]
            attended = dot(values.T, wbuf[sub], NN).astype(jnp.bfloat16)
            dout_t = head_rows(do_ref, slot, sub).T
            product = dout_t.astype(jnp.float32) * attended.astype(jnp.float32)
            delta[sub] = jnp.broadcast_to(jnp.sum(product, axis=0, keepdims=True), (8, QH * SUB))
            turned[sub] = dout_t
            store_heads(att_ref, slot, sub, attended.T)

    def backward(slot, place, order):
        for sub in order:
            low = max(place * CH, sub * SUB)
            high = min(place * CH + CH, sub * SUB + WIN)
            keys = kbuf[slot, low:high]
            values = vbuf[slot, low:high]
            weights = wbuf[sub, low - sub * SUB : high - sub * SUB]
            dprob = dot(values, turned[sub], NN)
            dscore = (weights.astype(jnp.float32) * (dprob - delta[sub][:1])).astype(jnp.bfloat16)
            grad_k = dot(dscore, head_rows(q_ref, slot, sub), NN)
            grad_v = dot(weights, head_rows(do_ref, slot, sub), NN)
            grad_q = dot(keys.T, dscore, NN)
            if sub == order[0]:
                acck[slot, low:high] = grad_k
                accv[slot, low:high] = grad_v
            else:
                acck[slot, low:high] = acck[slot, low:high] + grad_k
                accv[slot, low:high] = accv[slot, low:high] + grad_v
            if place == 0:
                accq[sub] = grad_q
            elif place == 1:
                accq[sub] = accq[sub] + grad_q
            else:
                grad_q = ((accq[sub] + grad_q) * SCALE).astype(jnp.bfloat16)
                store_heads(dq_ref, slot, sub, grad_q.T)

    def pack(slot, place):
        rows = slice(place * CH, (place + 1) * CH)
        gout[slot, place, :CH] = acck[slot, rows].astype(jnp.bfloat16)
        gout[slot, place, CH:] = accv[slot, rows].astype(jnp.bfloat16)

    def give_far(slot):
        pack(slot, 0)

        @pl.when(slot == other)
        def _():
            send_gf.start()

        start((slot == k) & near_u, send_gb)
        start((slot == k) & cross_u, send_gr)
        start((slot == k) & fold, send_gfold)

    def give_near(slot):
        @pl.when(slot == other)
        def _():
            pack(other, 1)
            send_gc.start()

    def give_sum(slot):
        @pl.when(slot == k)
        def _():
            send_gf.wait_recv()
            sum_k = acck[k, CH:OWN] + gfold[:CH].astype(jnp.float32)
            sum_v = accv[k, CH:OWN] + gfold[CH:].astype(jnp.float32)

            @pl.when(has_u)
            def _():
                gout[k, 1, :CH] = sum_k.astype(jnp.bfloat16)
                gout[k, 1, CH:] = sum_v.astype(jnp.bfloat16)
                send_ga.start()

            @pl.when(fold)
            def _():
                acck[0, OWN:] = acck[0, OWN:] + sum_k
                accv[0, OWN:] = accv[0, OWN:] + sum_v

    for copy in loads:
        copy.wait()

    def saves(slot):
        rows = pl.ds(slot * CH, CH)
        return [
            pltpu.make_async_copy(att_ref.at[rows], att_hbm.at[rows], save.at[2 * slot]),
            pltpu.make_async_copy(dq_ref.at[rows], dq_hbm.at[rows], save.at[2 * slot + 1]),
        ]

    early = (y < 2).astype(jnp.int32)

    def turn(index, carry):
        slot = early + index - 2 * early * index
        arrive(slot, kbuf, send_f[0], (AK, BK, CK, FK))
        send_far((index == 0) & (group == 1))
        weigh(slot)
        send_far((index == 0) & (group == 2))
        arrive(slot, vbuf, send_f[1], (AV, BV, CV, FV))
        attend(slot)
        send_far((index == 0) & (group == 3))
        backward(slot, 0, (0, 1, 2))
        give_far(slot)
        backward(slot, 1, (0, 1, 2))
        give_near(slot)
        backward(slot, 2, (2, 1, 0))
        give_sum(slot)
        for copy in saves(slot):
            copy.start()
        return carry

    lax.fori_loop(0, 2, turn, 0)

    @pl.when(relay_g)
    def _():
        for come, go in zip(send_gr, pass_g):
            come.wait_recv()
            go.start()

    def add(slot, which):
        acck[slot, OWN:] = acck[slot, OWN:] + gin[which, :CH].astype(jnp.float32)
        accv[slot, OWN:] = accv[slot, OWN:] + gin[which, CH:].astype(jnp.float32)

    send_gc.wait_recv()
    add(k, 2)

    @pl.when(has_u)
    def _():
        send_ga.wait_recv()
        add(other, 0)

    @pl.when(has_w | folded)
    def _():
        for copy in send_gb:
            copy.wait_recv()
        add(k, 1)

    for slot in range(2):
        rows = slice(slot * CH, (slot + 1) * CH)
        dk_ref[rows] = (acck[slot, OWN:] * SCALE).astype(jnp.bfloat16)
        dv_ref[rows] = accv[slot, OWN:].astype(jnp.bfloat16)

    last = [
        pltpu.make_async_copy(dk_ref, dk_hbm, save.at[4]),
        pltpu.make_async_copy(dv_ref, dv_hbm, save.at[5]),
    ]
    for copy in last:
        copy.start()

    def sent(when, copies):
        @pl.when(when)
        def _():
            for copy in copies:
                copy.wait_send()

    for copy in send_c + send_f + [send_gc, send_gf]:
        copy.wait_send()
    sent(has_u, send_a + [send_ga])
    sent(near_w, send_b)
    sent(cross_w, send_r)
    sent(relay_kv, pass_on)
    sent(near_u, send_gb)
    sent(cross_u, send_gr)
    sent(fold, send_gfold)
    sent(relay_g, pass_g)
    for copy in saves(0) + saves(1) + last:
        copy.wait()


def write(*refs):
    sources, outs, held, came, done = refs[:4], refs[4:8], refs[8:12], refs[12], refs[13]
    loads = [
        pltpu.make_async_copy(src, buf, came.at[i])
        for i, (src, buf) in enumerate(zip(sources, held))
    ]
    copies = [
        pltpu.make_async_copy(buf, out, done.at[i])
        for i, (buf, out) in enumerate(zip(held, outs))
    ]
    for copy in loads:
        copy.start()
    for load, copy in zip(loads, copies):
        load.wait()
        copy.start()
    for copy in copies:
        copy.wait()


def body(query, key, value, d_out, doc_lengths):
    rows, features = query.shape
    vmem = pl.BlockSpec(memory_space=pltpu.VMEM)
    hbm = pl.BlockSpec(memory_space=pltpu.HBM)
    bf16, f32 = jnp.bfloat16, jnp.float32
    shapes = [
        jax.ShapeDtypeStruct((rows, features), bf16),
        jax.ShapeDtypeStruct((rows, features), bf16),
        jax.ShapeDtypeStruct((rows, HD), bf16),
        jax.ShapeDtypeStruct((rows, HD), bf16),
    ]
    made = pl.pallas_call(
        kernel,
        out_shape=shapes,
        in_specs=[hbm] * 4 + [vmem],
        out_specs=[hbm] * 4,
        scratch_shapes=[
            *[pltpu.VMEM((rows, features), bf16)] * 4,
            *[pltpu.VMEM((rows, HD), bf16)] * 2,
            pltpu.VMEM((2, 3 * CH, HD), bf16),
            pltpu.VMEM((2, 3 * CH, HD), bf16),
            pltpu.VMEM((2, 3, 8, HD), jnp.int32),
            pltpu.VMEM((2, 3 * CH, HD), f32),
            pltpu.VMEM((2, 3 * CH, HD), f32),
            pltpu.VMEM((3, WIN, QH * SUB), bf16),
            pltpu.VMEM((3, 8, QH * SUB), f32),
            pltpu.VMEM((3, HD, QH * SUB), bf16),
            pltpu.VMEM((3, HD, QH * SUB), f32),
            pltpu.VMEM((2, 2, 2 * CH, HD), bf16),
            pltpu.VMEM((3, 2 * CH, HD), bf16),
            pltpu.VMEM((2 * CH, HD), bf16),
            pltpu.VMEM((2, CH, HD), bf16),
            pltpu.VMEM((2 * CH, HD), bf16),
            pltpu.SemaphoreType.DMA((COPIES,)),
            pltpu.SemaphoreType.DMA((COPIES,)),
            pltpu.SemaphoreType.DMA((4,)),
            pltpu.SemaphoreType.DMA((6,)),
            pltpu.SemaphoreType.DMA((6,)),
        ],
        compiler_params=pltpu.CompilerParams(
            collective_id=0, has_side_effects=True, vmem_limit_bytes=60_000_000
        ),
        cost_estimate=pl.CostEstimate(
            flops=4_300_000_000, bytes_accessed=4_000_000, transcendentals=2_800_000
        ),
    )(query, key, value, d_out, doc_lengths.reshape(1, -1))
    return pl.pallas_call(
        write,
        out_shape=shapes,
        in_specs=[hbm] * 4,
        out_specs=[hbm] * 4,
        scratch_shapes=[
            *[pltpu.VMEM(shape.shape, bf16) for shape in shapes],
            pltpu.SemaphoreType.DMA((4,)),
            pltpu.SemaphoreType.DMA((4,)),
        ],
        compiler_params=pltpu.CompilerParams(vmem_limit_bytes=60_000_000),
        cost_estimate=pl.CostEstimate(flops=0, bytes_accessed=4_000_000, transcendentals=0),
    )(*made)


def solution(mesh):
    wide = P(("dp", "ctx"), None)
    return jax.shard_map(
        body,
        mesh=mesh,
        in_specs=(wide, wide, wide, wide, P("dp")),
        out_specs=(wide, wide, wide, wide),
        check_vma=False,
    )
```

```python
import math

import jax
import jax.numpy as jnp
from jax import lax
from jax.experimental import pallas as pl
from jax.experimental.pallas import tpu as pltpu
from jax.sharding import PartitionSpec as P

HD = 128
QH = 4
CH = 384
SUB = 128
WIN = 7 * SUB
OWN = 2 * CH
CHIPS = 32
MASKED = -1e30
SCALE = 1.0 / math.sqrt(HD)
SCALE2 = SCALE * math.log2(math.e)
LATER = (3, 5, 8)
MESH = pl.DeviceIdType.MESH
NN = (((1,), (0,)), ((), ()))
AK, AV, BK, BV, CK, CV, FK, FV, RK, RV, GA, GB, HB, GC, GF, GR, HR, COPIES = range(18)


def dot(a, b, dims):
    return lax.dot_general(a, b, dims, preferred_element_type=jnp.float32)


def kernel(
    q_hbm, k_hbm, v_hbm, do_hbm, len_ref,
    att_hbm, dq_hbm, dk_hbm, dv_hbm,
    q_ref, do_ref, att_ref, dq_ref, dk_ref, dv_ref, kbuf, vbuf, first, acck, accv,
    wbuf, delta, mask, asked, turned, accq, gout, gin, gfold, relay, grelay, send, recv, fwd, load, save,
):
    d = lax.axis_index("ctx")
    c, k = d // 2, lax.rem(d, 2)
    y = lax.rem(c, 4)
    other = 1 - k
    step = 2 * k - 1
    u, w = c + step, c - step
    u2, w2 = c + 2 * step, c - 2 * step
    edge_u, edge_w = 3 * k, 3 * (1 - k)
    has_u = (u >= 0) & (u < CHIPS)
    has_w = (w >= 0) & (w < CHIPS)
    cross_u = has_u & (y == edge_u)
    cross_w = has_w & (y == edge_w)
    near_u = has_u & (y != edge_u)
    near_w = has_w & (y != edge_w)
    fold = (c == CHIPS - 1) & (k == 1)
    folded = (c == CHIPS - 1) & (k == 0)
    relay_kv = (y == edge_w + 1 - 2 * (1 - k)) & (w2 >= 0) & (w2 < CHIPS)
    relay_g = (y == edge_u + 1 - 2 * k) & (u2 >= 0) & (u2 < CHIPS)

    def at(chip, core):
        return {"ctx": chip * 2 + core}

    barrier = pltpu.get_barrier_semaphore()

    def greet(when, chip, core):
        @pl.when(when)
        def _():
            pl.semaphore_signal(barrier, inc=1, device_id=at(chip, core), device_id_type=MESH)

    pl.semaphore_signal(barrier, inc=1, device_id=at(c, other), device_id_type=MESH)
    greet(has_u, u, other)
    greet(near_u, u, k)
    greet(near_w, w, k)
    greet(cross_u, u2, k)
    greet(cross_w, w2, k)

    loads = [
        pltpu.make_async_copy(q_hbm, q_ref, load.at[0]),
        pltpu.make_async_copy(do_hbm, do_ref, load.at[1]),
    ]
    for slot in range(2):
        rows, place = pl.ds(slot * CH, CH), pl.ds(OWN, CH)
        loads += [
            pltpu.make_async_copy(k_hbm.at[rows], kbuf.at[slot, place], load.at[2 + 2 * slot]),
            pltpu.make_async_copy(v_hbm.at[rows], vbuf.at[slot, place], load.at[3 + 2 * slot]),
        ]
    for copy in loads:
        copy.start()

    @pl.when((c == 0) & (k == 0))
    def _():
        kbuf[0, :OWN] = jnp.zeros((OWN, HD), jnp.bfloat16)
        vbuf[0, :OWN] = jnp.zeros((OWN, HD), jnp.bfloat16)

    lens = jnp.broadcast_to(len_ref[...], (HD, HD))
    line = lax.broadcasted_iota(jnp.int32, (HD, HD), 0)
    lane = lax.broadcasted_iota(jnp.int32, (HD, HD), 1)
    starts = jnp.sum(
        jnp.where(lane < line, lens, 0).astype(jnp.float32), axis=1, keepdims=True
    ).astype(jnp.int32)
    for slot in range(2):
        block = d if slot == 0 else 2 * (2 * CHIPS) - 1 - d
        for sub in range(3):
            pos = block * CH + sub * SUB + lane
            held = jnp.where(starts <= pos, starts, 0)
            held = jnp.max(held.astype(jnp.float32), axis=0, keepdims=True).astype(jnp.int32)
            first[slot, sub] = jnp.broadcast_to(held - (block * CH - OWN + sub * SUB), (8, HD))

    count = (
        1
        + has_u.astype(jnp.int32)
        + near_u.astype(jnp.int32)
        + near_w.astype(jnp.int32)
        + relay_kv.astype(jnp.int32)
        + relay_g.astype(jnp.int32)
    )
    pl.semaphore_wait(barrier, count)

    def remote(src, dst, which, chip, core, out=None):
        return pltpu.make_async_remote_copy(
            src_ref=src,
            dst_ref=dst,
            send_sem=send.at[which] if out is None else out,
            recv_sem=recv.at[which],
            device_id=at(chip, core),
            device_id_type=MESH,
        )

    near, far = pl.ds(CH, CH), pl.ds(0, CH)
    mine, theirs = pl.ds(k * CH, CH), pl.ds(other * CH, CH)
    send_a = [
        remote(k_hbm.at[theirs], kbuf.at[other, near], AK, u, other),
        remote(v_hbm.at[theirs], vbuf.at[other, near], AV, u, other),
    ]
    send_b = [
        remote(k_hbm.at[mine], kbuf.at[k, far], BK, w, k),
        remote(v_hbm.at[mine], vbuf.at[k, far], BV, w, k),
    ]
    send_r = [
        remote(k_hbm.at[mine], relay.at[0], RK, u, k),
        remote(v_hbm.at[mine], relay.at[1], RV, u, k),
    ]
    send_c = [
        remote(k_hbm.at[mine], kbuf.at[k, near], CK, c, other),
        remote(v_hbm.at[mine], vbuf.at[k, near], CV, c, other),
    ]
    send_f = [
        remote(kbuf.at[k, near], kbuf.at[k, far], FK, c, other),
        remote(vbuf.at[k, near], vbuf.at[k, far], FV, c, other),
    ]
    pass_on = [
        remote(relay.at[0], kbuf.at[k, far], BK, w2, k, fwd.at[0]),
        remote(relay.at[1], vbuf.at[k, far], BV, w2, k, fwd.at[1]),
    ]
    send_ga = remote(gout.at[k, 1], gin.at[0], GA, u, other)
    halves = [pl.ds(0, CH), pl.ds(CH, CH)]
    send_gb = [remote(gout.at[k, 0, h], gin.at[1, h], GB + i, u, k) for i, h in enumerate(halves)]
    send_gfold = [
        remote(gout.at[k, 0, h], gin.at[1, h], GB + i, c, other) for i, h in enumerate(halves)
    ]
    send_gr = [remote(gout.at[k, 0, h], grelay.at[h], GR + i, w, k) for i, h in enumerate(halves)]
    send_gc = remote(gout.at[other, 1], gin.at[2], GC, c, other)
    send_gf = remote(gout.at[other, 0], gfold, GF, c, other)
    pass_g = [
        remote(grelay.at[h], gin.at[1, h], GB + i, u2, k, fwd.at[2 + i])
        for i, h in enumerate(halves)
    ]

    def start(when, copies):
        @pl.when(when)
        def _():
            for copy in copies:
                copy.start()

    z_low = lax.axis_index("dp")
    group = sum((z_low >= bound).astype(jnp.int32) for bound in LATER)

    def send_far(when):
        start(cross_u & when, send_a)

        @pl.when(relay_kv & when)
        def _():
            for come, go in zip(send_r, pass_on):
                come.wait_recv()
                go.start()

    start(near_u, send_a)
    start(cross_w, send_r)
    start(near_w, send_b)
    for copy in send_c:
        copy.start()
    send_far(group == 0)

    def landed(dst, which):
        remote(dst, dst, which, c, other).wait_recv()

    def arrive(slot, buf, copy_f, which):
        of_a, of_b, of_c, of_f = which

        @pl.when(slot == k)
        def _():
            @pl.when(fold)
            def _():
                buf[1, CH:OWN] = buf[0, OWN:]
                buf[1, :CH] = buf[0, CH:OWN]

            @pl.when(has_u)
            def _():
                landed(buf.at[k, near], of_a)

            copy_f.start()

            @pl.when(has_u)
            def _():
                landed(buf.at[k, far], of_b)

        @pl.when(slot == other)
        def _():
            landed(buf.at[other, near], of_c)
            landed(buf.at[other, far], of_f)

    def head_rows(ref, slot, sub):
        rows = pl.ds(pl.multiple_of(slot * CH + sub * SUB, SUB), SUB)
        return jnp.concatenate([ref[rows, h * HD : (h + 1) * HD] for h in range(QH)], axis=0)

    def store_heads(ref, slot, sub, value):
        rows = pl.ds(pl.multiple_of(slot * CH + sub * SUB, SUB), SUB)
        for h in range(QH):
            ref[rows, h * HD : (h + 1) * HD] = value[h * SUB : (h + 1) * SUB]

    def ready(slot):
        for sub in range(3):
            asked[sub] = head_rows(q_ref, slot, sub).T
            turned[sub] = head_rows(do_ref, slot, sub).T
            key_line = lax.broadcasted_iota(jnp.int32, (WIN, SUB), 0)
            query_lane = lax.broadcasted_iota(jnp.int32, (WIN, SUB), 1)
            allowed = (key_line - OWN <= query_lane) & (key_line >= first[slot, sub][:1])
            mask[sub] = jnp.where(allowed, 0.0, MASKED)

    def weigh(slot):
        for sub in range(3):
            keys = kbuf[slot, sub * SUB : sub * SUB + WIN]
            bias = jnp.concatenate([mask[sub]] * QH, axis=1)
            scores = dot(keys, asked[sub], NN) * SCALE2 + bias
            top = jnp.max(scores, axis=0, keepdims=True)
            raised = jnp.exp2(scores - top)
            total = jnp.sum(raised, axis=0, keepdims=True)
            wbuf[sub] = (raised * (1.0 / total)).astype(jnp.bfloat16)

    def attend(slot):
        for sub in range(3):
            values = vbuf[slot, sub * SUB : sub * SUB + WIN]
            attended = dot(values.T, wbuf[sub], NN).astype(jnp.bfloat16)
            product = turned[sub].astype(jnp.float32) * attended.astype(jnp.float32)
            delta[sub] = jnp.broadcast_to(jnp.sum(product, axis=0, keepdims=True), (8, QH * SUB))
            store_heads(att_ref, slot, sub, attended.T)

    def backward(slot, place, order):
        for sub in order:
            low = max(place * CH, sub * SUB)
            high = min(place * CH + CH, sub * SUB + WIN)
            keys = kbuf[slot, low:high]
            values = vbuf[slot, low:high]
            weights = wbuf[sub, low - sub * SUB : high - sub * SUB]
            dprob = dot(values, turned[sub], NN)
            dscore = (weights.astype(jnp.float32) * (dprob - delta[sub][:1])).astype(jnp.bfloat16)
            grad_k = dot(dscore, head_rows(q_ref, slot, sub), NN)
            grad_v = dot(weights, head_rows(do_ref, slot, sub), NN)
            grad_q = dot(keys.T, dscore, NN)
            if sub == order[0]:
                acck[slot, low:high] = grad_k
                accv[slot, low:high] = grad_v
            else:
                acck[slot, low:high] = acck[slot, low:high] + grad_k
                accv[slot, low:high] = accv[slot, low:high] + grad_v
            if place == 0:
                accq[sub] = grad_q
            elif place == 1:
                accq[sub] = accq[sub] + grad_q
            else:
                grad_q = ((accq[sub] + grad_q) * SCALE).astype(jnp.bfloat16)
                store_heads(dq_ref, slot, sub, grad_q.T)

    def pack(slot, place):
        rows = slice(place * CH, (place + 1) * CH)
        gout[slot, place, :CH] = acck[slot, rows].astype(jnp.bfloat16)
        gout[slot, place, CH:] = accv[slot, rows].astype(jnp.bfloat16)

    def give_far(slot):
        pack(slot, 0)

        @pl.when(slot == other)
        def _():
            send_gf.start()

        start((slot == k) & near_u, send_gb)
        start((slot == k) & cross_u, send_gr)
        start((slot == k) & fold, send_gfold)

    def give_near(slot):
        @pl.when(slot == other)
        def _():
            pack(other, 1)
            send_gc.start()

    def give_sum(slot):
        @pl.when(slot == k)
        def _():
            send_gf.wait_recv()
            sum_k = acck[k, CH:OWN] + gfold[:CH].astype(jnp.float32)
            sum_v = accv[k, CH:OWN] + gfold[CH:].astype(jnp.float32)

            @pl.when(has_u)
            def _():
                gout[k, 1, :CH] = sum_k.astype(jnp.bfloat16)
                gout[k, 1, CH:] = sum_v.astype(jnp.bfloat16)
                send_ga.start()

            @pl.when(fold)
            def _():
                acck[0, OWN:] = acck[0, OWN:] + sum_k
                accv[0, OWN:] = accv[0, OWN:] + sum_v

    for copy in loads:
        copy.wait()

    def saves(slot):
        rows = pl.ds(slot * CH, CH)
        return [
            pltpu.make_async_copy(att_ref.at[rows], att_hbm.at[rows], save.at[2 * slot]),
            pltpu.make_async_copy(dq_ref.at[rows], dq_hbm.at[rows], save.at[2 * slot + 1]),
        ]

    early = (y < 2).astype(jnp.int32)

    def turn(index, carry):
        slot = early + index - 2 * early * index
        ready(slot)
        arrive(slot, kbuf, send_f[0], (AK, BK, CK, FK))
        send_far((index == 0) & (group == 1))
        weigh(slot)
        send_far((index == 0) & (group == 2))
        arrive(slot, vbuf, send_f[1], (AV, BV, CV, FV))
        attend(slot)
        send_far((index == 0) & (group == 3))
        backward(slot, 0, (0, 1, 2))
        give_far(slot)
        backward(slot, 1, (0, 1, 2))
        give_near(slot)
        backward(slot, 2, (2, 1, 0))
        give_sum(slot)
        for copy in saves(slot):
            copy.start()
        return carry

    lax.fori_loop(0, 2, turn, 0)

    @pl.when(relay_g)
    def _():
        for come, go in zip(send_gr, pass_g):
            come.wait_recv()
            go.start()

    def add(slot, which):
        acck[slot, OWN:] = acck[slot, OWN:] + gin[which, :CH].astype(jnp.float32)
        accv[slot, OWN:] = accv[slot, OWN:] + gin[which, CH:].astype(jnp.float32)

    send_gc.wait_recv()
    add(k, 2)

    def finish(slot):
        rows = pl.ds(pl.multiple_of(slot * CH, SUB), CH)
        dk_ref[rows] = (acck[slot, OWN:] * SCALE).astype(jnp.bfloat16)
        dv_ref[rows] = accv[slot, OWN:].astype(jnp.bfloat16)
        for copy in last(slot):
            copy.start()

    def last(slot):
        rows = pl.ds(pl.multiple_of(slot * CH, SUB), CH)
        return [
            pltpu.make_async_copy(dk_ref.at[rows], dk_hbm.at[rows], save.at[4 + 2 * slot]),
            pltpu.make_async_copy(dv_ref.at[rows], dv_hbm.at[rows], save.at[5 + 2 * slot]),
        ]

    @pl.when(has_u)
    def _():
        send_ga.wait_recv()
        add(other, 0)

    finish(other)

    @pl.when(has_w | folded)
    def _():
        for copy in send_gb:
            copy.wait_recv()
        add(k, 1)

    finish(k)

    def sent(when, copies):
        @pl.when(when)
        def _():
            for copy in copies:
                copy.wait_send()

    for copy in send_c + send_f + [send_gc, send_gf]:
        copy.wait_send()
    sent(has_u, send_a + [send_ga])
    sent(near_w, send_b)
    sent(cross_w, send_r)
    sent(relay_kv, pass_on)
    sent(near_u, send_gb)
    sent(cross_u, send_gr)
    sent(fold, send_gfold)
    sent(relay_g, pass_g)
    for copy in saves(0) + saves(1) + last(0) + last(1):
        copy.wait()


def write(*refs):
    sources, outs, held, came, done = refs[:4], refs[4:8], refs[8:12], refs[12], refs[13]
    loads = [
        pltpu.make_async_copy(src, buf, came.at[i])
        for i, (src, buf) in enumerate(zip(sources, held))
    ]
    copies = [
        pltpu.make_async_copy(buf, out, done.at[i])
        for i, (buf, out) in enumerate(zip(held, outs))
    ]
    for copy in loads:
        copy.start()
    for load, copy in zip(loads, copies):
        load.wait()
        copy.start()
    for copy in copies:
        copy.wait()


def body(query, key, value, d_out, doc_lengths):
    rows, features = query.shape
    vmem = pl.BlockSpec(memory_space=pltpu.VMEM)
    hbm = pl.BlockSpec(memory_space=pltpu.HBM)
    bf16, f32 = jnp.bfloat16, jnp.float32
    shapes = [
        jax.ShapeDtypeStruct((rows, features), bf16),
        jax.ShapeDtypeStruct((rows, features), bf16),
        jax.ShapeDtypeStruct((rows, HD), bf16),
        jax.ShapeDtypeStruct((rows, HD), bf16),
    ]
    made = pl.pallas_call(
        kernel,
        out_shape=shapes,
        in_specs=[hbm] * 4 + [vmem],
        out_specs=[hbm] * 4,
        scratch_shapes=[
            *[pltpu.VMEM((rows, features), bf16)] * 4,
            *[pltpu.VMEM((rows, HD), bf16)] * 2,
            pltpu.VMEM((2, 3 * CH, HD), bf16),
            pltpu.VMEM((2, 3 * CH, HD), bf16),
            pltpu.VMEM((2, 3, 8, HD), jnp.int32),
            pltpu.VMEM((2, 3 * CH, HD), f32),
            pltpu.VMEM((2, 3 * CH, HD), f32),
            pltpu.VMEM((3, WIN, QH * SUB), bf16),
            pltpu.VMEM((3, 8, QH * SUB), f32),
            pltpu.VMEM((3, WIN, SUB), f32),
            pltpu.VMEM((3, HD, QH * SUB), bf16),
            pltpu.VMEM((3, HD, QH * SUB), bf16),
            pltpu.VMEM((3, HD, QH * SUB), f32),
            pltpu.VMEM((2, 2, 2 * CH, HD), bf16),
            pltpu.VMEM((3, 2 * CH, HD), bf16),
            pltpu.VMEM((2 * CH, HD), bf16),
            pltpu.VMEM((2, CH, HD), bf16),
            pltpu.VMEM((2 * CH, HD), bf16),
            pltpu.SemaphoreType.DMA((COPIES,)),
            pltpu.SemaphoreType.DMA((COPIES,)),
            pltpu.SemaphoreType.DMA((4,)),
            pltpu.SemaphoreType.DMA((6,)),
            pltpu.SemaphoreType.DMA((8,)),
        ],
        compiler_params=pltpu.CompilerParams(
            collective_id=0, has_side_effects=True, vmem_limit_bytes=60_000_000
        ),
        cost_estimate=pl.CostEstimate(
            flops=4_300_000_000, bytes_accessed=4_000_000, transcendentals=2_800_000
        ),
    )(query, key, value, d_out, doc_lengths.reshape(1, -1))
    return pl.pallas_call(
        write,
        out_shape=shapes,
        in_specs=[hbm] * 4,
        out_specs=[hbm] * 4,
        scratch_shapes=[
            *[pltpu.VMEM(shape.shape, bf16) for shape in shapes],
            pltpu.SemaphoreType.DMA((4,)),
            pltpu.SemaphoreType.DMA((4,)),
        ],
        compiler_params=pltpu.CompilerParams(vmem_limit_bytes=60_000_000),
        cost_estimate=pl.CostEstimate(flops=0, bytes_accessed=4_000_000, transcendentals=0),
    )(*made)


def solution(mesh):
    wide = P(("dp", "ctx"), None)
    return jax.shard_map(
        body,
        mesh=mesh,
        in_specs=(wide, wide, wide, wide, P("dp")),
        out_specs=(wide, wide, wide, wide),
        check_vma=False,
    )
```
